256 devices in a mesh: fsdp: 32 (over z_lo, y, x), tok: 8 (over z_hi, core).
Axes of the slice: x: 4, y: 4, z: 8 (z_hi: 4, z_lo: 2; z = z_hi * 2 + z_lo), core: 2. Of those that a mesh axis runs over, the one named last changes fastest.
Arguments:
- tokens: bfloat16 [1024, 8192], P(None, 'tok'), may hold values from -6 to 6
- gate_a: bfloat16 [14336, 8192], P('fsdp', 'tok'), may hold values from -0.0625 to 0.0625
- up_a: bfloat16 [14336, 8192], P('fsdp', 'tok'), may hold values from -0.0625 to 0.0625
- gate_b: bfloat16 [14336, 8192], P('fsdp', 'tok'), may hold values from -0.0625 to 0.0625
- up_b: bfloat16 [14336, 8192], P('fsdp', 'tok'), may hold values from -0.0625 to 0.0625
- matching: int32 [14336], replicated, may hold values from 0 to 14335, as said below
- mixing: float32 [14336], P('fsdp'), may hold values from 0.2 to 0.8
Outputs:
- correlation: bfloat16 [14336, 14336], P('fsdp', 'tok')
- merged_gate: bfloat16 [14336, 8192], P('fsdp', 'tok')
- merged_up: bfloat16 [14336, 8192], P('fsdp', 'tok')
The draws below stay inside these ranges and needn't reach their ends.
Inputs may be any that keep to these rules, and one draw needn't show every extreme that they name: A permutation of the 14336 units, found in an earlier round by an assignment limited in capacity, so that every block of 448 consecutive positions holds exactly 14 entries from each block of 448 consecutive values. The correlation computed here feeds the next round's matching.
All inputs are finite; a program needn't handle non-finite values.
Results may differ from the reference program's by a relative error of at most 0.0057.
Values may be sent and summed in bfloat16 or wider, within the bound.
A program may use at most 128 MiB of HBM per device.

```python
import math
import jax
import jax.numpy as jnp

D = 8192
FF = 14336
TOKENS = 1024
R = 448
CAP = 14
N_FSDP = 32


def draw_matching(key, part):
    key = jax.random.fold_in(key, 11)
    first, second = jax.random.split(key)
    inner = jax.vmap(lambda subkey: jax.random.permutation(subkey, R))(jax.random.split(first, N_FSDP))
    target = jnp.arange(N_FSDP)[:, None, None]
    anchor = jnp.arange(N_FSDP)[None, :, None]
    within = jnp.arange(CAP)[None, None, :]
    picked = anchor * R + inner[anchor, target * CAP + within]
    picked = picked.reshape(N_FSDP, R)
    shuffle = jax.vmap(lambda subkey: jax.random.permutation(subkey, R))(jax.random.split(second, N_FSDP))
    placed = jnp.take_along_axis(picked, shuffle, axis=1)
    return placed.reshape(FF).astype(jnp.int32)


def steps_of(key, dims, cuts, least, largest):
    def one(position, blocks):
        heights = jax.random.uniform(jax.random.fold_in(jax.random.fold_in(key, 6), position), (blocks,), jnp.float32, least / len(cuts), largest / len(cuts))
        return jnp.repeat(jnp.exp(heights), dims[position] // blocks).reshape((-1,) + (1,) * (len(dims) - position - 1))

    factor_of = one(*cuts[0])
    for cut in cuts[1:]:
        factor_of = factor_of * one(*cut)
    return factor_of


def centred(rng, shape, deviation, most, cuts=(), dtype=jnp.bfloat16):
    drawn = deviation * jax.random.normal(rng, shape, jnp.float32)
    if cuts:
        drawn = drawn * steps_of(rng, shape, cuts, -0.22, 0.18)
    return jnp.clip(drawn, -most, most).astype(dtype)


def setup_inputs(seed: int = 0) -> dict:
    keys = jax.random.split(jax.random.key(seed), 8)
    tokens = centred(keys[0], (TOKENS, D), 1.0, 6.0, ((1, 8),))
    gate_a = centred(keys[1], (FF, D), D ** -0.5, 0.0625, ((0, 32), (1, 8)))
    up_a = centred(keys[2], (FF, D), D ** -0.5, 0.0625, ((0, 32), (1, 8)))
    gate_b = centred(keys[3], (FF, D), D ** -0.5, 0.0625, ((0, 32), (1, 8)))
    up_b = centred(keys[4], (FF, D), D ** -0.5, 0.0625, ((0, 32), (1, 8)))
    matching = draw_matching(jax.random.fold_in(keys[7], 71), 0)
    mixing = jnp.clip(0.2 + 0.6 * jax.random.uniform(keys[6], (FF,), jnp.float32) ** steps_of(keys[6], (FF,), ((0, 32),), -0.2, 0.2), 0.2, 0.8)
    return {"tokens": tokens, "gate_a": gate_a, "up_a": up_a, "gate_b": gate_b, "up_b": up_b, "matching": matching, "mixing": mixing}


def activation(tokens, gate, up_proj):
    gate_pre = jnp.dot(tokens, gate.T, preferred_element_type=jnp.float32)
    up_pre = jnp.dot(tokens, up_proj.T, preferred_element_type=jnp.float32)
    return (jax.nn.silu(gate_pre) * up_pre).astype(jnp.bfloat16)

def blend_rows(own_rows, other_rows, mixing):
    weight = mixing[:, None]
    mixed = (1.0 - weight) * own_rows.astype(jnp.float32) + weight * other_rows.astype(jnp.float32)
    return mixed.astype(jnp.bfloat16)

def reference(tokens, gate_a, up_a, gate_b, up_b, matching, mixing):
    act_a = activation(tokens, gate_a, up_a)
    act_b = activation(tokens, gate_b, up_b)
    summed = jnp.dot(act_a.T, act_b, preferred_element_type=jnp.float32)
    correlation = (summed / math.sqrt(TOKENS)).astype(jnp.bfloat16)
    matched_gate = jnp.take(gate_b, matching, axis=0)
    matched_up = jnp.take(up_b, matching, axis=0)
    merged_gate = blend_rows(gate_a, matched_gate, mixing)
    merged_up = blend_rows(up_a, matched_up, mixing)
    return (correlation, merged_gate, merged_up)
```

```python
import math

import jax
import jax.numpy as jnp
from jax import lax
from jax.experimental import pallas as pl
from jax.experimental.pallas import tpu as pltpu
from jax.sharding import PartitionSpec as P

MESH = pl.DeviceIdType.MESH
BF16, F32 = jnp.bfloat16, jnp.float32
UNITS = 448
HALF = UNITS // 2
WIDTH = 1024
QUARTER = 256
SLOTS = 16
NT = (((1,), (1,)), ((), ()))


def device(x, y, l, h, c):
    return (l * 16 + y * 4 + x, h * 2 + c)


def remote(src, dst, send, recv, to):
    return pltpu.make_async_remote_copy(
        src_ref=src, dst_ref=dst, send_sem=send, recv_sem=recv, device_id=to, device_id_type=MESH
    )


def rows(start, size, step):
    return pl.ds(pl.multiple_of(start, step), size)


def kernel(
    tok, gate_a, up_a, gate_b, up_b, send_rows, position, mixing,
    corr, merged_gate, merged_up,
    tk, wh, wb, wa, outb, inb, sb, rb, pa, pb, po, ab, aa, bb, acc, corr_v, mg_v, onehot,
    l_sem, xs_sem, xr_sem, as_sem, ar_sem, rs_s, rs_r, b1_s, b1_r, b2_s, b2_r, b3_s, b3_r,
    az_s, az_r, ac_s, ac_r, o_sem,
):
    f, t = lax.axis_index("fsdp"), lax.axis_index("tok")
    x, y, l = lax.rem(f, 4), lax.rem(lax.div(f, 4), 4), lax.div(f, 16)
    h, c = lax.div(t, 2), lax.rem(t, 2)
    weights = (gate_a, up_a, gate_b, up_b)
    order = [lax.rem(h + d, 4) for d in (2, 1, 3, 0)]

    loads = []
    for i, w in enumerate(weights):
        loads.append(
            pltpu.make_async_copy(
                w.at[rows(c * HALF, HALF, HALF)], wh.at[c, pl.ds(i * HALF, HALF)], l_sem.at[i]
            )
        )
    loads.append(pltpu.make_async_copy(tok, tk.at[c], l_sem.at[4]))
    loads_b = [
        pltpu.make_async_copy(w, wb.at[i], l_sem.at[5 + i]) for i, w in enumerate((gate_b, up_b))
    ]
    loads_a = [
        pltpu.make_async_copy(w, wa.at[i], l_sem.at[7 + i]) for i, w in enumerate((gate_a, up_a))
    ]
    for cp in loads + loads_b + loads_a:
        cp.start()

    barrier = pltpu.get_barrier_semaphore()

    def greet_f(i, carry):
        pl.semaphore_signal(
            barrier, inc=1, device_id=(lax.rem(f + i, 32), t), device_id_type=MESH
        )
        return carry

    def greet_t(i, carry):
        other = lax.rem(t + i, 8)
        pl.semaphore_signal(barrier, inc=1, device_id=(f, other), device_id_type=MESH)
        pl.semaphore_signal(
            barrier, inc=1, device_id=(lax.rem(f + 16, 32), other), device_id_type=MESH
        )
        return carry

    lax.fori_loop(1, 32, greet_f, 0)
    lax.fori_loop(1, 8, greet_t, 0)
    pl.semaphore_wait(barrier, 45)

    sibling = (f, t + 1 - 2 * c)
    swaps = []
    for i, w in enumerate(weights):
        swaps.append(
            remote(
                w.at[rows((1 - c) * HALF, HALF, HALF)],
                wh.at[c, pl.ds(i * HALF, HALF)],
                xs_sem.at[i],
                xr_sem.at[i],
                sibling,
            )
        )
    for i, e in enumerate(order):
        part = rows(e * QUARTER, QUARTER, QUARTER)
        swaps.append(
            remote(tok.at[part], tk.at[c, part], xs_sem.at[4 + i], xr_sem.at[4 + i], sibling)
        )
    for cp in swaps:
        cp.start()

    onehot[...] = (
        lax.broadcasted_iota(jnp.int32, (32 * SLOTS, UNITS), 1) == send_rows[...]
    ).astype(F32).astype(BF16)
    for i in range(2):
        loads_b[i].wait()
        picked = jnp.dot(onehot[...], wb[i], preferred_element_type=F32).astype(BF16)
        outb[:, i * SLOTS : (i + 1) * SLOTS, :] = picked.reshape(32, SLOTS, WIDTH)

    own_rows = pltpu.make_async_copy(outb.at[f], inb.at[f], l_sem.at[9])
    own_rows.start()

    def a2a(i):
        to = lax.rem(f + i, 32)
        return remote(outb.at[to], inb.at[f], as_sem.at[i], ar_sem.at[i], (to, t))

    def a2a_in(i):
        frm = lax.rem(f + 32 - i, 32)
        return remote(outb.at[frm], inb.at[frm], as_sem.at[i], ar_sem.at[i], (frm, t))

    def plane_step(i, carry):
        to = l * 16 + lax.rem(lax.rem(f, 16) + i, 16)
        a2a(lax.rem(to - f + 32, 32)).start()
        return carry

    def cross_step(i, carry):
        to = (1 - l) * 16 + lax.rem(lax.rem(f, 16) + i, 16)
        a2a(lax.rem(to - f + 32, 32)).start()
        return carry

    lax.fori_loop(1, 16, plane_step, 0)

    for cp in loads:
        cp.wait()
    for cp in swaps[:4]:
        cp.wait_recv()

    def partial(i):
        swaps[4 + i].wait_recv()
        part = rows(order[i] * QUARTER, QUARTER, QUARTER)
        return lax.dot_general(
            wh[0], tk[0, part, :], NT, preferred_element_type=F32
        ) + lax.dot_general(wh[1], tk[1, part, :], NT, preferred_element_type=F32)

    plus = device(x, y, l, lax.rem(h + 1, 4), c)
    minus = device(x, y, l, lax.rem(h + 3, 4), c)

    def ring(i, to):
        return remote(sb.at[i], rb.at[i], rs_s.at[i], rs_r.at[i], to)

    far_a, far_b, near_b, near_a = ring(0, plus), ring(1, minus), ring(2, plus), ring(3, minus)
    acc_a, acc_b = ring(4, plus), ring(5, minus)

    p = partial(0)
    sb[1] = p[UNITS:].astype(BF16)
    far_b.start()
    sb[0] = p[:UNITS].astype(BF16)
    far_a.start()
    p = partial(1)
    sb[2] = p[UNITS:].astype(BF16)
    near_b.start()
    pa[...] = p[:UNITS]
    p = partial(2)
    sb[3] = p[:UNITS].astype(BF16)
    near_a.start()
    pb[...] = p[UNITS:]
    po[...] = partial(3)
    far_b.wait_recv()
    sb[5] = (pb[...] + rb[1].astype(F32)).astype(BF16)
    acc_b.start()
    far_a.wait_recv()
    sb[4] = (pa[...] + rb[0].astype(F32)).astype(BF16)
    acc_a.start()

    lax.fori_loop(0, 16, cross_step, 0)

    def activation(lo, first, second):
        total = po[lo : lo + UNITS, :] + rb[first].astype(F32) + rb[second].astype(F32)
        gate, up = total[:HALF], total[HALF:]
        return ((gate / (1.0 + jnp.exp(-gate))) * up).astype(BF16)

    near_b.wait_recv()
    acc_b.wait_recv()
    ab[...] = activation(UNITS, 2, 5)
    slab, side = 2 * l + lax.div(y, 2), lax.rem(y, 2)
    mine = rows(x * UNITS + c * HALF, HALF, HALF)
    b1_slot = h * 2 + c
    to_root = remote(
        ab, bb.at[h, mine], b1_s.at[0], b1_r.at[b1_slot], device(x, y, l, slab, side)
    )
    to_twin = remote(
        ab, bb.at[h, mine], b1_s.at[1], b1_r.at[b1_slot], device(x, y, 1 - l, slab, side)
    )
    is_self = jnp.logical_and(slab == h, side == c)
    to_twin.start()

    @pl.when(jnp.logical_not(is_self))
    def _():
        to_root.start()

    @pl.when(is_self)
    def _():
        pltpu.make_async_copy(ab, bb.at[h, mine], b1_r.at[b1_slot]).start()

    near_a.wait_recv()
    acc_a.wait_recv()
    half = rows(c * HALF, HALF, HALF)
    aa[h, half, :] = activation(0, 3, 4)
    a_out = [
        remote(
            aa.at[h, half], aa.at[h, half], az_s.at[d], az_r.at[d],
            device(x, y, l, lax.rem(h + d, 4), c),
        )
        for d in (1, 3, 2)
    ]
    for cp in a_out:
        cp.start()

    def a_in(d):
        frm = lax.rem(h + 4 - d, 4)
        return remote(
            aa.at[frm, half], aa.at[frm, half], az_s.at[d], az_r.at[d], device(x, y, l, frm, c)
        )

    def relay(d):
        frm = lax.rem(h + 4 - d, 4)
        return remote(aa.at[frm, half], aa.at[frm, half], ac_s.at[d], ac_r.at[d], sibling)

    def relay_in(d):
        frm = lax.rem(h + 4 - d, 4)
        other = rows((1 - c) * HALF, HALF, HALF)
        return remote(aa.at[frm, other], aa.at[frm, other], ac_s.at[d], ac_r.at[d], sibling)

    relay(0).start()

    is_root = y == 2 * lax.rem(h, 2) + c
    right = device(lax.rem(x + 1, 4), y, l, h, c)
    left = device(lax.rem(x + 3, 4), y, l, h, c)
    quarters = [lax.rem(h + d, 4) for d in (0, 1, 3, 2)]

    def block(q, dx):
        return bb.at[q, rows(lax.rem(x + dx, 4) * UNITS, UNITS, UNITS)]

    def down(s, dy):
        here = block(quarters[s], 0)
        return remote(
            here, here, b2_s.at[s, dy - 1], b2_r.at[s], device(x, lax.rem(y + dy, 4), l, h, c)
        )

    def to_right(s):
        here = block(quarters[s], 0)
        return remote(here, here, b3_s.at[s, 0], b3_r.at[s, 0], right)

    def to_left(s):
        here = block(quarters[s], 0)
        return remote(here, here, b3_s.at[s, 1], b3_r.at[s, 1], left)

    def from_left(s):
        there = block(quarters[s], 3)
        return remote(there, there, b3_s.at[s, 0], b3_r.at[s, 0], left)

    def from_right(s):
        there = block(quarters[s], 1)
        return remote(there, there, b3_s.at[s, 1], b3_r.at[s, 1], right)

    def forward(s):
        there = block(quarters[s], 3 if s % 2 == 0 else 1)
        return remote(there, there, b3_s.at[s, 2], b3_r.at[s, 2], right if s % 2 == 0 else left)

    def from_far(s):
        there = block(quarters[s], 2)
        return remote(there, there, b3_s.at[s, 2], b3_r.at[s, 2], left if s % 2 == 0 else right)

    def b1_in(s, core):
        q = quarters[s]
        here = bb.at[q, rows(x * UNITS + core * HALF, HALF, HALF)]
        return pltpu.make_async_copy(here, here, b1_r.at[q * 2 + core])

    def correlate(s):
        term = lax.dot_general(
            aa[quarters[s]], bb[quarters[s]], NT, preferred_element_type=F32
        )
        if s == 0:
            acc[...] = term
        elif s < 3:
            acc[...] += term
        else:
            corr_v[...] = ((acc[...] + term) * (1.0 / 32.0)).astype(BF16)

    relayed = [0, 3, 1, 2]
    for step in range(6):
        if step < 4:

            @pl.when(is_root)
            def _():
                b1_in(step, 0).wait()
                b1_in(step, 1).wait()
                for dy in (1, 3, 2):
                    down(step, dy).start()

            @pl.when(jnp.logical_not(is_root))
            def _():
                down(step, 1).wait_recv()

            to_right(step).start()
            to_left(step).start()
        if step == 1:
            for d in (1, 3):
                a_in(d).wait_recv()
                relay(d).start()
        if step == 2:
            a_in(2).wait_recv()
            relay(2).start()
        if 1 <= step < 5:
            from_left(step - 1).wait_recv()
            from_right(step - 1).wait_recv()
            forward(step - 1).start()
        if step == 5:
            own_rows.wait()

            def arrived(i, carry):
                a2a_in(i).wait_recv()
                return carry

            lax.fori_loop(1, 32, arrived, 0)
            for cp in loads_a:
                cp.wait()
            weight = mixing[...]
            lane = lax.broadcasted_iota(jnp.int32, (UNITS, 32 * 2 * SLOTS), 1)
            received = inb[...].reshape(32 * 2 * SLOTS, WIDTH)
            for i, out in enumerate((merged_gate, merged_up)):
                pick = (lane == position[...] + i * SLOTS).astype(F32).astype(BF16)
                got = jnp.dot(pick, received, preferred_element_type=F32)
                mg_v[i] = ((1.0 - weight) * wa[i].astype(F32) + weight * got).astype(BF16)
                pltpu.make_async_copy(mg_v.at[i], out, o_sem.at[i]).start()
        if step >= 2:
            if step == 2:
                relay_in(0).wait_recv()
                for d in (1, 3, 2):
                    relay_in(d).wait_recv()
            from_far(step - 2).wait_recv()
            correlate(step - 2)

    out = pltpu.make_async_copy(corr_v, corr, o_sem.at[2])
    out.start()

    for cp in swaps + [far_a, far_b, near_a, near_b, acc_a, acc_b, to_twin] + a_out:
        cp.wait_send()

    @pl.when(jnp.logical_not(is_self))
    def _():
        to_root.wait_send()

    for s in range(4):

        @pl.when(is_root)
        def _():
            for dy in (1, 3, 2):
                down(s, dy).wait_send()

        to_right(s).wait_send()
        to_left(s).wait_send()
        forward(s).wait_send()
        relay(s).wait_send()

    def left_all(i, carry):
        a2a(i).wait_send()
        return carry

    lax.fori_loop(1, 32, left_all, 0)
    pltpu.make_async_copy(mg_v.at[0], merged_gate, o_sem.at[0]).wait()
    pltpu.make_async_copy(mg_v.at[1], merged_up, o_sem.at[1]).wait()
    out.wait()


def body(tokens, gate_a, up_a, gate_b, up_b, matching, mixing):
    count = lax.axis_size("fsdp")
    own = lax.axis_index("fsdp")
    table = matching.reshape(count, UNITS)
    chosen = (table // UNITS == own).astype(jnp.int32)
    slot = jnp.cumsum(chosen, axis=1) - 1
    hits = jnp.logical_and(
        chosen[:, None, :] > 0, slot[:, None, :] == jnp.arange(SLOTS)[None, :, None]
    )
    send_rows = jnp.sum(jnp.where(hits, (table % UNITS)[:, None, :], 0), axis=2).reshape(-1, 1)
    wanted = lax.dynamic_slice_in_dim(matching, own * UNITS, UNITS, 0)
    anchor = wanted // UNITS
    same = (anchor[:, None] == jnp.arange(count)[None, :]).astype(jnp.int32)
    rank = jnp.sum(same * (jnp.cumsum(same, axis=0) - 1), axis=1)
    position = (anchor * (2 * SLOTS) + rank).reshape(-1, 1)

    any_space = pl.BlockSpec(memory_space=pl.ANY)
    vmem = pl.BlockSpec(memory_space=pltpu.VMEM)
    dma = pltpu.SemaphoreType.DMA
    return pl.pallas_call(
        kernel,
        name="match_merge",
        out_shape=(
            jax.ShapeDtypeStruct((UNITS, 4 * UNITS), BF16),
            jax.ShapeDtypeStruct((UNITS, WIDTH), BF16),
            jax.ShapeDtypeStruct((UNITS, WIDTH), BF16),
        ),
        in_specs=[any_space] * 5 + [vmem] * 3,
        out_specs=(any_space,) * 3,
        scratch_shapes=[
            pltpu.VMEM((2, 1024, WIDTH), BF16),
            pltpu.VMEM((2, 4 * HALF, WIDTH), BF16),
            pltpu.VMEM((2, UNITS, WIDTH), BF16),
            pltpu.VMEM((2, UNITS, WIDTH), BF16),
            pltpu.VMEM((32, 2 * SLOTS, WIDTH), BF16),
            pltpu.VMEM((32, 2 * SLOTS, WIDTH), BF16),
            pltpu.VMEM((6, UNITS, QUARTER), BF16),
            pltpu.VMEM((6, UNITS, QUARTER), BF16),
            pltpu.VMEM((UNITS, QUARTER), F32),
            pltpu.VMEM((UNITS, QUARTER), F32),
            pltpu.VMEM((2 * UNITS, QUARTER), F32),
            pltpu.VMEM((HALF, QUARTER), BF16),
            pltpu.VMEM((4, UNITS, QUARTER), BF16),
            pltpu.VMEM((4, 4 * UNITS, QUARTER), BF16),
            pltpu.VMEM((UNITS, 4 * UNITS), F32),
            pltpu.VMEM((UNITS, 4 * UNITS), BF16),
            pltpu.VMEM((2, UNITS, WIDTH), BF16),
            pltpu.VMEM((32 * SLOTS, UNITS), BF16),
            dma((10,)),
            dma((8,)),
            dma((8,)),
            dma((32,)),
            dma((32,)),
            dma((6,)),
            dma((6,)),
            dma((2,)),
            dma((8,)),
            dma((4, 3)),
            dma((4,)),
            dma((4, 3)),
            dma((4, 3)),
            dma((4,)),
            dma((4,)),
            dma((4,)),
            dma((4,)),
            dma((3,)),
        ],
        compiler_params=pltpu.CompilerParams(
            collective_id=0, has_side_effects=True, vmem_limit_bytes=56 * 2**20
        ),
        cost_estimate=pl.CostEstimate(
            flops=8_000_000_000, bytes_accessed=20_000_000, transcendentals=500_000
        ),
    )(tokens, gate_a, up_a, gate_b, up_b, send_rows, position, mixing.reshape(-1, 1))


def solution(mesh):
    placed = (
        P(None, "tok"),
        P("fsdp", "tok"),
        P("fsdp", "tok"),
        P("fsdp", "tok"),
        P("fsdp", "tok"),
        P(),
        P("fsdp"),
    )
    return jax.shard_map(
        body,
        mesh=mesh,
        in_specs=placed,
        out_specs=(P("fsdp", "tok"), P("fsdp", "tok"), P("fsdp", "tok")),
        check_vma=False,
    )
```

```python
import jax
import jax.numpy as jnp
from jax import lax
from jax.experimental import pallas as pl
from jax.experimental.pallas import tpu as pltpu
from jax.sharding import PartitionSpec as P

MESH = pl.DeviceIdType.MESH
BF16, F32 = jnp.bfloat16, jnp.float32
UNITS = 448
HALF = UNITS // 2
WIDTH = 1024
QUARTER = 256
SLOTS = 16
NT = (((1,), (1,)), ((), ()))


def device(x, y, l, h, c):
    return (l * 16 + y * 4 + x, h * 2 + c)


def remote(src, dst, send, recv, to):
    return pltpu.make_async_remote_copy(
        src_ref=src, dst_ref=dst, send_sem=send, recv_sem=recv, device_id=to, device_id_type=MESH
    )


def rows(start, size, step):
    return pl.ds(pl.multiple_of(start, step), size)


def kernel(
    tok, gate_a, up_a, gate_b, up_b, table, mixing,
    corr, merged_gate, merged_up,
    tk, wh, wb, wa, outb, near_in, twin_in, sb, rb, keep, ab, aa, bb, acc, corr_v, mg_v,
    send_hot, take_hot, line, column,
    l_sem, xs_s, xs_r, as_s, as_r, fw_s, fw_r, rs_s, rs_r, b1_s, b1_r, b2_s, b2_r, b3_s, b3_r,
    az_s, az_r, ac_s, ac_r, o_sem,
):
    f, t = lax.axis_index("fsdp"), lax.axis_index("tok")
    x, y, l = lax.rem(f, 4), lax.rem(lax.div(f, 4), 4), lax.div(f, 16)
    h, c = lax.div(t, 2), lax.rem(t, 2)
    xy = lax.rem(f, 16)
    weights = (gate_b, up_b, gate_a, up_a)
    order = [lax.rem(h + d, 4) for d in (2, 1, 3, 0)]
    sibling = (f, t + 1 - 2 * c)
    twin = device(x, y, 1 - l, h, c)

    barrier = pltpu.get_barrier_semaphore()

    def greet_plane(i, carry):
        pl.semaphore_signal(
            barrier, inc=1, device_id=(l * 16 + lax.rem(xy + i, 16), t), device_id_type=MESH
        )
        return carry

    def greet_tok(i, carry):
        other = lax.rem(t + i, 8)
        pl.semaphore_signal(barrier, inc=1, device_id=(f, other), device_id_type=MESH)
        pl.semaphore_signal(
            barrier, inc=1, device_id=((1 - l) * 16 + xy, other), device_id_type=MESH
        )
        return carry

    lax.fori_loop(1, 16, greet_plane, 0)
    lax.fori_loop(1, 8, greet_tok, 0)
    pl.semaphore_signal(barrier, inc=1, device_id=twin, device_id_type=MESH)

    loads = []
    for i, w in enumerate(weights):
        loads.append(
            pltpu.make_async_copy(
                w.at[rows(c * HALF, HALF, HALF)], wh.at[c, pl.ds(i * HALF, HALF)], l_sem.at[i]
            )
        )
    load_tok = pltpu.make_async_copy(tok, tk.at[c], l_sem.at[4])
    loads_b = [
        pltpu.make_async_copy(w, wb.at[i], l_sem.at[5 + i]) for i, w in enumerate((gate_b, up_b))
    ]
    loads_a = [
        pltpu.make_async_copy(w, wa.at[i], l_sem.at[7 + i]) for i, w in enumerate((gate_a, up_a))
    ]
    for cp in loads_b + loads[:2] + [load_tok] + loads[2:] + loads_a:
        cp.start()

    low = f * UNITS
    value = table[...]
    local = value - low
    chosen = jnp.logical_and(local >= 0, local < UNITS)
    source = lax.broadcasted_iota(jnp.int32, (32, UNITS), 0)
    wanted = table[pl.ds(f, 1), :] - source * UNITS
    same = jnp.logical_and(wanted >= 0, wanted < UNITS)
    before = (
        lax.broadcasted_iota(jnp.int32, (UNITS, UNITS), 0)
        < lax.broadcasted_iota(jnp.int32, (UNITS, UNITS), 1)
    ).astype(F32).astype(BF16)
    chosen_f, same_f = chosen.astype(F32), same.astype(F32)
    rank = jnp.dot(chosen_f.astype(BF16), before, preferred_element_type=F32)
    rank_in = jnp.dot(same_f.astype(BF16), before, preferred_element_type=F32)
    base = (lax.rem(source + 16 * l, 32) * SLOTS).astype(F32)
    line[...] = jnp.zeros_like(line)
    line[0:1, 0:UNITS] = jnp.sum(same_f * (base + rank_in), axis=0, keepdims=True)
    line[1:2, 0:UNITS] = mixing[...]
    column[...] = line[...].T
    take_hot[...] = (
        lax.broadcasted_iota(jnp.int32, (UNITS, 32 * SLOTS), 1)
        == column[0:UNITS, 0:1].astype(jnp.int32)
    ).astype(F32).astype(BF16)
    slot_row = lax.broadcasted_iota(jnp.int32, (32 * SLOTS, 32), 0)
    to_block = lax.rem(lax.broadcasted_iota(jnp.int32, (32 * SLOTS, 32), 1) + 16 * l, 32)
    spread = (lax.shift_right_logical(slot_row, 4) == to_block).astype(F32).astype(BF16)

    def widen(v):
        return jnp.dot(spread, v.astype(BF16), preferred_element_type=F32)

    code = widen(chosen_f * (rank + 1.0) - 1.0)
    high = widen(chosen_f * lax.shift_right_arithmetic(local, 4).astype(F32))
    lowp = widen(chosen_f * jnp.bitwise_and(local, 15).astype(F32))
    slot = jnp.bitwise_and(
        lax.broadcasted_iota(jnp.int32, (32 * SLOTS, UNITS), 0), SLOTS - 1
    ).astype(F32)
    picked_row = jnp.sum(
        jnp.where(code == slot, high * 16.0 + lowp, 0.0), axis=1, keepdims=True
    ).astype(jnp.int32)
    send_hot[...] = (
        lax.broadcasted_iota(jnp.int32, (32 * SLOTS, UNITS), 1) == picked_row
    ).astype(F32).astype(BF16)

    pl.semaphore_wait(barrier, 30)

    swaps = []
    for i, w in enumerate(weights):
        swaps.append(
            remote(
                w.at[rows((1 - c) * HALF, HALF, HALF)],
                wh.at[c, pl.ds(i * HALF, HALF)],
                xs_s.at[i],
                xs_r.at[i],
                sibling,
            )
        )
    for i, e in enumerate(order):
        part = rows(e * QUARTER, QUARTER, QUARTER)
        swaps.append(
            remote(tok.at[part], tk.at[c, part], xs_s.at[4 + i], xs_r.at[4 + i], sibling)
        )
    for i in (0, 1, 4, 5, 6, 7, 2, 3):
        swaps[i].start()

    for i in range(2):
        loads_b[i].wait()
        picked = jnp.dot(send_hot[...], wb[i], preferred_element_type=F32).astype(BF16)
        outb[:, 0, i] = picked[: 16 * SLOTS].reshape(16, SLOTS, WIDTH)
        outb[:, 1, i] = picked[16 * SLOTS :].reshape(16, SLOTS, WIDTH)

    def plane(i):
        to = lax.rem(xy + i, 16)
        return remote(outb.at[to], near_in.at[xy], as_s.at[i], as_r.at[i], (l * 16 + to, t))

    def plane_in(i):
        frm = lax.rem(xy + 16 - i, 16)
        return remote(outb.at[frm], near_in.at[frm], as_s.at[i], as_r.at[i], (l * 16 + frm, t))

    def plane_step(i, carry):
        plane(i).start()
        return carry

    own_rows = pltpu.make_async_copy(outb.at[xy, 0], near_in.at[xy, 0], l_sem.at[9])
    own_rows.start()
    own_cross = remote(outb.at[xy, 1], twin_in.at[xy], fw_s.at[0], fw_r.at[0], twin)
    lax.fori_loop(1, 16, plane_step, 0)

    plus = device(x, y, l, lax.rem(h + 1, 4), c)
    minus = device(x, y, l, lax.rem(h + 3, 4), c)

    def ring(k, i):
        return remote(
            sb.at[k, i], rb.at[k, i], rs_s.at[k, i], rs_r.at[k, i], plus if i % 2 == 0 else minus
        )

    def partial(k, i):
        part = rows(order[i] * QUARTER, QUARTER, QUARTER)
        mine = slice(k * UNITS, (k + 1) * UNITS)
        return lax.dot_general(
            wh[0, mine], tk[0, part, :], NT, preferred_element_type=F32
        ) + lax.dot_general(wh[1, mine], tk[1, part, :], NT, preferred_element_type=F32)

    def push(k, i, v):
        sb[k, i] = v.astype(BF16)
        ring(k, i).start()

    for cp in loads[:2] + [load_tok]:
        cp.wait()
    for i in (0, 1, 4):
        swaps[i].wait_recv()
    p = partial(0, 0)
    push(0, 0, p[:HALF])
    push(0, 1, p[HALF:])
    swaps[5].wait_recv()
    p = partial(0, 1)
    push(0, 2, p[HALF:])
    keep[0, 0] = p[:HALF]
    swaps[6].wait_recv()
    p = partial(0, 2)
    push(0, 3, p[:HALF])
    keep[0, 1] = p[HALF:]
    swaps[7].wait_recv()
    p = partial(0, 3)
    keep[0, 2] = p[:HALF]
    keep[0, 3] = p[HALF:]
    for cp in loads[2:]:
        cp.wait()
    for i in (2, 3):
        swaps[i].wait_recv()
    p = partial(1, 0)
    sb[1, 0] = p[:HALF].astype(BF16)
    sb[1, 1] = p[HALF:].astype(BF16)
    for i in range(2):
        ring(0, i).wait_recv()
        push(0, 4 + i, keep[0, i] + rb[0, i].astype(F32))
    ring(1, 0).start()
    ring(1, 1).start()
    p = partial(1, 1)
    push(1, 2, p[HALF:])
    keep[1, 0] = p[:HALF]
    p = partial(1, 2)
    push(1, 3, p[:HALF])
    keep[1, 1] = p[HALF:]
    p = partial(1, 3)
    keep[1, 2] = p[:HALF]
    keep[1, 3] = p[HALF:]

    def activation(k):
        for i in range(2, 6):
            ring(k, i).wait_recv()
        gate = keep[k, 2] + rb[k, 3].astype(F32) + rb[k, 4].astype(F32)
        up = keep[k, 3] + rb[k, 2].astype(F32) + rb[k, 5].astype(F32)
        return ((gate / (1.0 + jnp.exp(-gate))) * up).astype(BF16)

    ab[...] = activation(0)
    slab, side = 2 * l + lax.div(y, 2), lax.rem(y, 2)
    mine = rows(x * UNITS + c * HALF, HALF, HALF)
    b1_slot = h * 2 + c
    to_root = remote(
        ab, bb.at[h, mine], b1_s.at[0], b1_r.at[b1_slot], device(x, y, l, slab, side)
    )
    to_twin = remote(
        ab, bb.at[h, mine], b1_s.at[1], b1_r.at[b1_slot], device(x, y, 1 - l, slab, side)
    )
    is_self = jnp.logical_and(slab == h, side == c)
    to_twin.start()

    @pl.when(jnp.logical_not(is_self))
    def _():
        to_root.start()

    @pl.when(is_self)
    def _():
        pltpu.make_async_copy(ab, bb.at[h, mine], b1_r.at[b1_slot]).start()

    for i in range(2):
        ring(1, i).wait_recv()
        push(1, 4 + i, keep[1, i] + rb[1, i].astype(F32))

    half = rows(c * HALF, HALF, HALF)
    a_out = [
        remote(
            aa.at[h, half], aa.at[h, half], az_s.at[d], az_r.at[d],
            device(x, y, l, lax.rem(h + d, 4), c),
        )
        for d in (1, 3, 2)
    ]

    def a_in(d):
        frm = lax.rem(h + 4 - d, 4)
        return remote(
            aa.at[frm, half], aa.at[frm, half], az_s.at[d], az_r.at[d], device(x, y, l, frm, c)
        )

    def relay(d):
        frm = lax.rem(h + 4 - d, 4)
        return remote(aa.at[frm, half], aa.at[frm, half], ac_s.at[d], ac_r.at[d], sibling)

    def relay_in(d):
        frm = lax.rem(h + 4 - d, 4)
        other = rows((1 - c) * HALF, HALF, HALF)
        return remote(aa.at[frm, other], aa.at[frm, other], ac_s.at[d], ac_r.at[d], sibling)

    is_root = y == 2 * lax.rem(h, 2) + c
    right = device(lax.rem(x + 1, 4), y, l, h, c)
    left = device(lax.rem(x + 3, 4), y, l, h, c)
    quarters = [lax.rem(h + d, 4) for d in (0, 1, 3, 2)]

    def block(q, dx):
        return bb.at[q, rows(lax.rem(x + dx, 4) * UNITS, UNITS, UNITS)]

    def down(s, dy):
        here = block(quarters[s], 0)
        return remote(
            here, here, b2_s.at[s, dy - 1], b2_r.at[s], device(x, lax.rem(y + dy, 4), l, h, c)
        )

    def to_right(s):
        here = block(quarters[s], 0)
        return remote(here, here, b3_s.at[s, 0], b3_r.at[s, 0], right)

    def to_left(s):
        here = block(quarters[s], 0)
        return remote(here, here, b3_s.at[s, 1], b3_r.at[s, 1], left)

    def from_left(s):
        there = block(quarters[s], 3)
        return remote(there, there, b3_s.at[s, 0], b3_r.at[s, 0], left)

    def from_right(s):
        there = block(quarters[s], 1)
        return remote(there, there, b3_s.at[s, 1], b3_r.at[s, 1], right)

    def forward(s):
        there = block(quarters[s], 3 if s % 2 == 0 else 1)
        return remote(there, there, b3_s.at[s, 2], b3_r.at[s, 2], right if s % 2 == 0 else left)

    def from_far(s):
        there = block(quarters[s], 2)
        return remote(there, there, b3_s.at[s, 2], b3_r.at[s, 2], left if s % 2 == 0 else right)

    def b1_in(s, core):
        q = quarters[s]
        here = bb.at[q, rows(x * UNITS + core * HALF, HALF, HALF)]
        return pltpu.make_async_copy(here, here, b1_r.at[q * 2 + core])

    def correlate(s):
        term = lax.dot_general(
            aa[quarters[s]], bb[quarters[s]], NT, preferred_element_type=F32
        )
        if s == 0:
            acc[...] = term
        elif s < 3:
            acc[...] += term
        else:
            corr_v[...] = ((acc[...] + term) * (1.0 / 32.0)).astype(BF16)

    def spread_out(s):
        @pl.when(is_root)
        def _():
            b1_in(s, 0).wait()
            b1_in(s, 1).wait()
            for dy in (1, 3, 2):
                down(s, dy).start()

        @pl.when(jnp.logical_not(is_root))
        def _():
            down(s, 1).wait_recv()

        to_right(s).start()
        to_left(s).start()

    def pass_on(s):
        from_left(s).wait_recv()
        from_right(s).wait_recv()
        forward(s).start()

    def cross(i):
        frm = lax.rem(xy + 16 - i, 16)
        return remote(near_in.at[frm, 1], twin_in.at[frm], fw_s.at[i], fw_r.at[i], twin)

    def cross_step(i, carry):
        plane_in(i).wait_recv()
        cross(i).start()
        return carry

    spread_out(0)
    aa[h, half, :] = activation(1)
    for cp in a_out:
        cp.start()
    relay(0).start()
    spread_out(1)
    pass_on(0)
    own_cross.start()
    lax.fori_loop(1, 16, cross_step, 0)
    spread_out(2)
    for d in (1, 3):
        a_in(d).wait_recv()
        relay(d).start()
    pass_on(1)
    a_in(2).wait_recv()
    relay(2).start()
    spread_out(3)
    pass_on(2)
    for d in range(4):
        relay_in(d).wait_recv()
    from_far(0).wait_recv()
    correlate(0)
    from_far(1).wait_recv()
    correlate(1)
    pass_on(3)
    from_far(2).wait_recv()
    correlate(2)

    own_rows.wait()

    def arrived(i, carry):
        cross(i).wait_recv()
        return carry

    own_cross.wait_recv()
    lax.fori_loop(1, 16, arrived, 0)
    for cp in loads_a:
        cp.wait()
    weight = column[0:UNITS, 1:2]
    outs = []
    for i, out in enumerate((merged_gate, merged_up)):
        got = jnp.dot(
            take_hot[:, : 16 * SLOTS],
            near_in[:, 0, i].reshape(16 * SLOTS, WIDTH),
            preferred_element_type=F32,
        ) + jnp.dot(
            take_hot[:, 16 * SLOTS :],
            twin_in[:, i].reshape(16 * SLOTS, WIDTH),
            preferred_element_type=F32,
        )
        mg_v[i] = ((1.0 - weight) * wa[i].astype(F32) + weight * got).astype(BF16)
        outs.append(pltpu.make_async_copy(mg_v.at[i], out, o_sem.at[i]))
        outs[-1].start()

    from_far(3).wait_recv()
    correlate(3)
    outs.append(pltpu.make_async_copy(corr_v, corr, o_sem.at[2]))
    outs[-1].start()

    for cp in swaps + [to_twin, own_cross] + a_out:
        cp.wait_send()
    for k in range(2):
        for i in range(6):
            ring(k, i).wait_send()

    @pl.when(jnp.logical_not(is_self))
    def _():
        to_root.wait_send()

    for s in range(4):

        @pl.when(is_root)
        def _():
            for dy in (1, 3, 2):
                down(s, dy).wait_send()

        to_right(s).wait_send()
        to_left(s).wait_send()
        forward(s).wait_send()
        relay(s).wait_send()

    def left_all(i, carry):
        plane(i).wait_send()
        cross(i).wait_send()
        return carry

    lax.fori_loop(1, 16, left_all, 0)
    for cp in outs:
        cp.wait()


def body(tokens, gate_a, up_a, gate_b, up_b, matching, mixing):
    any_space = pl.BlockSpec(memory_space=pl.ANY)
    vmem = pl.BlockSpec(memory_space=pltpu.VMEM)
    dma = pltpu.SemaphoreType.DMA
    return pl.pallas_call(
        kernel,
        name="match_merge",
        out_shape=(
            jax.ShapeDtypeStruct((UNITS, 4 * UNITS), BF16),
            jax.ShapeDtypeStruct((UNITS, WIDTH), BF16),
            jax.ShapeDtypeStruct((UNITS, WIDTH), BF16),
        ),
        in_specs=[any_space] * 5 + [vmem] * 2,
        out_specs=(any_space,) * 3,
        scratch_shapes=[
            pltpu.VMEM((2, 1024, WIDTH), BF16),
            pltpu.VMEM((2, 4 * HALF, WIDTH), BF16),
            pltpu.VMEM((2, UNITS, WIDTH), BF16),
            pltpu.VMEM((2, UNITS, WIDTH), BF16),
            pltpu.VMEM((16, 2, 2, SLOTS, WIDTH), BF16),
            pltpu.VMEM((16, 2, 2, SLOTS, WIDTH), BF16),
            pltpu.VMEM((16, 2, SLOTS, WIDTH), BF16),
            pltpu.VMEM((2, 6, HALF, QUARTER), BF16),
            pltpu.VMEM((2, 6, HALF, QUARTER), BF16),
            pltpu.VMEM((2, 4, HALF, QUARTER), F32),
            pltpu.VMEM((HALF, QUARTER), BF16),
            pltpu.VMEM((4, UNITS, QUARTER), BF16),
            pltpu.VMEM((4, 4 * UNITS, QUARTER), BF16),
            pltpu.VMEM((UNITS, 4 * UNITS), F32),
            pltpu.VMEM((UNITS, 4 * UNITS), BF16),
            pltpu.VMEM((2, UNITS, WIDTH), BF16),
            pltpu.VMEM((32 * SLOTS, UNITS), BF16),
            pltpu.VMEM((UNITS, 32 * SLOTS), BF16),
            pltpu.VMEM((8, 512), F32),
            pltpu.VMEM((512, 8), F32),
            dma((10,)),
            dma((8,)),
            dma((8,)),
            dma((16,)),
            dma((16,)),
            dma((16,)),
            dma((16,)),
            dma((2, 6)),
            dma((2, 6)),
            dma((2,)),
            dma((8,)),
            dma((4, 3)),
            dma((4,)),
            dma((4, 3)),
            dma((4, 3)),
            dma((4,)),
            dma((4,)),
            dma((4,)),
            dma((4,)),
            dma((3,)),
        ],
        compiler_params=pltpu.CompilerParams(
            collective_id=0, has_side_effects=True, vmem_limit_bytes=56 * 2**20
        ),
        cost_estimate=pl.CostEstimate(
            flops=8_000_000_000, bytes_accessed=20_000_000, transcendentals=500_000
        ),
    )(tokens, gate_a, up_a, gate_b, up_b, matching.reshape(32, UNITS), mixing.reshape(1, UNITS))


def solution(mesh):
    placed = (
        P(None, "tok"),
        P("fsdp", "tok"),
        P("fsdp", "tok"),
        P("fsdp", "tok"),
        P("fsdp", "tok"),
        P(),
        P("fsdp"),
    )
    return jax.shard_map(
        body,
        mesh=mesh,
        in_specs=placed,
        out_specs=(P("fsdp", "tok"), P("fsdp", "tok"), P("fsdp", "tok")),
        check_vma=False,
    )
```

```python
import jax
import jax.numpy as jnp
from jax import lax
from jax.experimental import pallas as pl
from jax.experimental.pallas import tpu as pltpu
from jax.sharding import PartitionSpec as P

MESH = pl.DeviceIdType.MESH
BF16, F32 = jnp.bfloat16, jnp.float32
UNITS = 448
HALF = UNITS // 2
WIDTH = 1024
QUARTER = 256
SLOTS = 16
NT = (((1,), (1,)), ((), ()))


def device(x, y, l, h, c):
    return (l * 16 + y * 4 + x, h * 2 + c)


def remote(src, dst, send, recv, to):
    return pltpu.make_async_remote_copy(
        src_ref=src, dst_ref=dst, send_sem=send, recv_sem=recv, device_id=to, device_id_type=MESH
    )


def rows(start, size, step):
    return pl.ds(pl.multiple_of(start, step), size)


def kernel(
    tok, gate_a, up_a, gate_b, up_b, table, mixing,
    corr, merged_gate, merged_up,
    tk, wh, wb, wa, outb, near_in, twin_in, sb, rb, keep, ab, aa, bb, acc, corr_v, mg_v,
    send_hot, take_hot, line, column, blocks,
    l_sem, xs_s, xs_r, as_s, as_r, fw_s, fw_r, rs_s, rs_r, b1_s, b1_r, b2_s, b2_r, b3_s, b3_r,
    az_s, az_r, ac_s, ac_r, o_sem,
):
    f, t = lax.axis_index("fsdp"), lax.axis_index("tok")
    x, y, l = lax.rem(f, 4), lax.rem(lax.div(f, 4), 4), lax.div(f, 16)
    h, c = lax.div(t, 2), lax.rem(t, 2)
    xy = lax.rem(f, 16)
    weights = (gate_b, up_b, gate_a, up_a)
    order = [lax.rem(h + d, 4) for d in (2, 1, 3, 0)]
    sibling = (f, t + 1 - 2 * c)
    twin = device(x, y, 1 - l, h, c)

    barrier = pltpu.get_barrier_semaphore()

    def greet_plane(i, carry):
        pl.semaphore_signal(
            barrier, inc=1, device_id=(l * 16 + lax.rem(xy + i, 16), t), device_id_type=MESH
        )
        return carry

    def greet_tok(i, carry):
        other = lax.rem(t + i, 8)
        pl.semaphore_signal(barrier, inc=1, device_id=(f, other), device_id_type=MESH)
        pl.semaphore_signal(
            barrier, inc=1, device_id=((1 - l) * 16 + xy, other), device_id_type=MESH
        )
        return carry

    lax.fori_loop(1, 16, greet_plane, 0)
    lax.fori_loop(1, 8, greet_tok, 0)
    pl.semaphore_signal(barrier, inc=1, device_id=twin, device_id_type=MESH)

    loads = []
    for i, w in enumerate(weights):
        loads.append(
            pltpu.make_async_copy(
                w.at[rows(c * HALF, HALF, HALF)], wh.at[c, pl.ds(i * HALF, HALF)], l_sem.at[i]
            )
        )
    load_tok = pltpu.make_async_copy(tok, tk.at[c], l_sem.at[4])
    loads_b = [
        pltpu.make_async_copy(w, wb.at[i], l_sem.at[5 + i]) for i, w in enumerate((gate_b, up_b))
    ]
    loads_a = [
        pltpu.make_async_copy(w, wa.at[i], l_sem.at[7 + i]) for i, w in enumerate((gate_a, up_a))
    ]
    for cp in loads_b + loads[:2] + [load_tok] + loads[2:] + loads_a:
        cp.start()

    strips = [table[pl.ds(i, 16, stride=7), :] for i in range(7)]
    blocks[0:16, :] = jnp.concatenate(strips[0:4], axis=1)[:, :UNITS]
    blocks[16:32, :] = jnp.concatenate(strips[3:7], axis=1)[:, 4 * 128 - UNITS :]
    low = f * UNITS
    value = blocks[...]
    local = value - low
    chosen = jnp.logical_and(local >= 0, local < UNITS)
    source = lax.broadcasted_iota(jnp.int32, (32, UNITS), 0)
    wanted = blocks[pl.ds(lax.div(f, 2) + 16 * lax.rem(f, 2), 1), :] - source * UNITS
    same = jnp.logical_and(wanted >= 0, wanted < UNITS)
    before = (
        lax.broadcasted_iota(jnp.int32, (UNITS, UNITS), 0)
        < lax.broadcasted_iota(jnp.int32, (UNITS, UNITS), 1)
    ).astype(F32).astype(BF16)
    chosen_f, same_f = chosen.astype(F32), same.astype(F32)
    rank = jnp.dot(chosen_f.astype(BF16), before, preferred_element_type=F32)
    rank_in = jnp.dot(same_f.astype(BF16), before, preferred_element_type=F32)
    base = (lax.rem(source + 16 * l, 32) * SLOTS).astype(F32)
    line[...] = jnp.zeros_like(line)
    line[0:1, 0:UNITS] = jnp.sum(same_f * (base + rank_in), axis=0, keepdims=True)
    line[1:2, 0:UNITS] = mixing[...]
    column[...] = line[...].T
    take_hot[...] = (
        lax.broadcasted_iota(jnp.int32, (UNITS, 32 * SLOTS), 1)
        == column[0:UNITS, 0:1].astype(jnp.int32)
    ).astype(F32).astype(BF16)
    slot_row = lax.broadcasted_iota(jnp.int32, (32 * SLOTS, 32), 0)
    held = lax.broadcasted_iota(jnp.int32, (32 * SLOTS, 32), 1)
    held = 2 * jnp.bitwise_and(held, 15) + lax.shift_right_logical(held, 4)
    to_block = lax.rem(held + 16 * l, 32)
    spread = (lax.shift_right_logical(slot_row, 4) == to_block).astype(F32).astype(BF16)

    def widen(v):
        return jnp.dot(spread, v.astype(BF16), preferred_element_type=F32)

    code = widen(chosen_f * (rank + 1.0) - 1.0)
    high = widen(chosen_f * lax.shift_right_arithmetic(local, 4).astype(F32))
    lowp = widen(chosen_f * jnp.bitwise_and(local, 15).astype(F32))
    slot = jnp.bitwise_and(
        lax.broadcasted_iota(jnp.int32, (32 * SLOTS, UNITS), 0), SLOTS - 1
    ).astype(F32)
    picked_row = jnp.sum(
        jnp.where(code == slot, high * 16.0 + lowp, 0.0), axis=1, keepdims=True
    ).astype(jnp.int32)
    send_hot[...] = (
        lax.broadcasted_iota(jnp.int32, (32 * SLOTS, UNITS), 1) == picked_row
    ).astype(F32).astype(BF16)

    pl.semaphore_wait(barrier, 30)

    swaps = []
    for i, w in enumerate(weights):
        swaps.append(
            remote(
                w.at[rows((1 - c) * HALF, HALF, HALF)],
                wh.at[c, pl.ds(i * HALF, HALF)],
                xs_s.at[i],
                xs_r.at[i],
                sibling,
            )
        )
    for i, e in enumerate(order):
        part = rows(e * QUARTER, QUARTER, QUARTER)
        swaps.append(
            remote(tok.at[part], tk.at[c, part], xs_s.at[4 + i], xs_r.at[4 + i], sibling)
        )
    for i in (0, 1, 4, 5, 6, 7, 2, 3):
        swaps[i].start()

    for i in range(2):
        loads_b[i].wait()
        picked = jnp.dot(send_hot[...], wb[i], preferred_element_type=F32).astype(BF16)
        outb[:, 0, i] = picked[: 16 * SLOTS].reshape(16, SLOTS, WIDTH)
        outb[:, 1, i] = picked[16 * SLOTS :].reshape(16, SLOTS, WIDTH)

    def plane(i):
        to = lax.rem(xy + i, 16)
        return remote(outb.at[to], near_in.at[xy], as_s.at[i], as_r.at[i], (l * 16 + to, t))

    def plane_in(i):
        frm = lax.rem(xy + 16 - i, 16)
        return remote(outb.at[frm], near_in.at[frm], as_s.at[i], as_r.at[i], (l * 16 + frm, t))

    def plane_step(i, carry):
        plane(i).start()
        return carry

    own_rows = pltpu.make_async_copy(outb.at[xy, 0], near_in.at[xy, 0], l_sem.at[9])
    own_rows.start()
    own_cross = remote(outb.at[xy, 1], twin_in.at[xy], fw_s.at[0], fw_r.at[0], twin)
    lax.fori_loop(1, 16, plane_step, 0)

    plus = device(x, y, l, lax.rem(h + 1, 4), c)
    minus = device(x, y, l, lax.rem(h + 3, 4), c)

    def ring(k, i):
        return remote(
            sb.at[k, i], rb.at[k, i], rs_s.at[k, i], rs_r.at[k, i], plus if i % 2 == 0 else minus
        )

    def partial(k, i):
        part = rows(order[i] * QUARTER, QUARTER, QUARTER)
        mine = slice(k * UNITS, (k + 1) * UNITS)
        return lax.dot_general(
            wh[0, mine], tk[0, part, :], NT, preferred_element_type=F32
        ) + lax.dot_general(wh[1, mine], tk[1, part, :], NT, preferred_element_type=F32)

    def push(k, i, v):
        sb[k, i] = v.astype(BF16)
        ring(k, i).start()

    for cp in loads[:2] + [load_tok]:
        cp.wait()
    for i in (0, 1, 4):
        swaps[i].wait_recv()
    p = partial(0, 0)
    push(0, 0, p[:HALF])
    push(0, 1, p[HALF:])
    swaps[5].wait_recv()
    p = partial(0, 1)
    push(0, 2, p[HALF:])
    keep[0, 0] = p[:HALF]
    swaps[6].wait_recv()
    p = partial(0, 2)
    push(0, 3, p[:HALF])
    keep[0, 1] = p[HALF:]
    swaps[7].wait_recv()
    p = partial(0, 3)
    keep[0, 2] = p[:HALF]
    keep[0, 3] = p[HALF:]
    for cp in loads[2:]:
        cp.wait()
    for i in (2, 3):
        swaps[i].wait_recv()
    p = partial(1, 0)
    sb[1, 0] = p[:HALF].astype(BF16)
    sb[1, 1] = p[HALF:].astype(BF16)
    for i in range(2):
        ring(0, i).wait_recv()
        push(0, 4 + i, keep[0, i] + rb[0, i].astype(F32))
    ring(1, 0).start()
    ring(1, 1).start()
    p = partial(1, 1)
    push(1, 2, p[HALF:])
    keep[1, 0] = p[:HALF]
    p = partial(1, 2)
    push(1, 3, p[:HALF])
    keep[1, 1] = p[HALF:]
    p = partial(1, 3)
    keep[1, 2] = p[:HALF]
    keep[1, 3] = p[HALF:]

    def activation(k):
        for i in range(2, 6):
            ring(k, i).wait_recv()
        gate = keep[k, 2] + rb[k, 3].astype(F32) + rb[k, 4].astype(F32)
        up = keep[k, 3] + rb[k, 2].astype(F32) + rb[k, 5].astype(F32)
        return ((gate / (1.0 + jnp.exp(-gate))) * up).astype(BF16)

    ab[...] = activation(0)
    slab, side = 2 * l + lax.div(y, 2), lax.rem(y, 2)
    mine = rows(x * UNITS + c * HALF, HALF, HALF)
    b1_slot = h * 2 + c
    to_root = remote(
        ab, bb.at[h, mine], b1_s.at[0], b1_r.at[b1_slot], device(x, y, l, slab, side)
    )
    to_twin = remote(
        ab, bb.at[h, mine], b1_s.at[1], b1_r.at[b1_slot], device(x, y, 1 - l, slab, side)
    )
    is_self = jnp.logical_and(slab == h, side == c)
    to_twin.start()

    @pl.when(jnp.logical_not(is_self))
    def _():
        to_root.start()

    @pl.when(is_self)
    def _():
        pltpu.make_async_copy(ab, bb.at[h, mine], b1_r.at[b1_slot]).start()

    for i in range(2):
        ring(1, i).wait_recv()
        push(1, 4 + i, keep[1, i] + rb[1, i].astype(F32))

    half = rows(c * HALF, HALF, HALF)
    a_out = [
        remote(
            aa.at[h, half], aa.at[h, half], az_s.at[d], az_r.at[d],
            device(x, y, l, lax.rem(h + d, 4), c),
        )
        for d in (1, 3, 2)
    ]

    def a_in(d):
        frm = lax.rem(h + 4 - d, 4)
        return remote(
            aa.at[frm, half], aa.at[frm, half], az_s.at[d], az_r.at[d], device(x, y, l, frm, c)
        )

    def relay(d):
        frm = lax.rem(h + 4 - d, 4)
        return remote(aa.at[frm, half], aa.at[frm, half], ac_s.at[d], ac_r.at[d], sibling)

    def relay_in(d):
        frm = lax.rem(h + 4 - d, 4)
        other = rows((1 - c) * HALF, HALF, HALF)
        return remote(aa.at[frm, other], aa.at[frm, other], ac_s.at[d], ac_r.at[d], sibling)

    is_root = y == 2 * lax.rem(h, 2) + c
    right = device(lax.rem(x + 1, 4), y, l, h, c)
    left = device(lax.rem(x + 3, 4), y, l, h, c)
    quarters = [lax.rem(h + d, 4) for d in (0, 1, 3, 2)]

    def block(q, dx):
        return bb.at[q, rows(lax.rem(x + dx, 4) * UNITS, UNITS, UNITS)]

    def down(s, dy):
        here = block(quarters[s], 0)
        return remote(
            here, here, b2_s.at[s, dy - 1], b2_r.at[s], device(x, lax.rem(y + dy, 4), l, h, c)
        )

    def to_right(s):
        here = block(quarters[s], 0)
        return remote(here, here, b3_s.at[s, 0], b3_r.at[s, 0], right)

    def to_left(s):
        here = block(quarters[s], 0)
        return remote(here, here, b3_s.at[s, 1], b3_r.at[s, 1], left)

    def from_left(s):
        there = block(quarters[s], 3)
        return remote(there, there, b3_s.at[s, 0], b3_r.at[s, 0], left)

    def from_right(s):
        there = block(quarters[s], 1)
        return remote(there, there, b3_s.at[s, 1], b3_r.at[s, 1], right)

    def forward(s):
        there = block(quarters[s], 3 if s % 2 == 0 else 1)
        return remote(there, there, b3_s.at[s, 2], b3_r.at[s, 2], right if s % 2 == 0 else left)

    def from_far(s):
        there = block(quarters[s], 2)
        return remote(there, there, b3_s.at[s, 2], b3_r.at[s, 2], left if s % 2 == 0 else right)

    def b1_in(s, core):
        q = quarters[s]
        here = bb.at[q, rows(x * UNITS + core * HALF, HALF, HALF)]
        return pltpu.make_async_copy(here, here, b1_r.at[q * 2 + core])

    def correlate(s):
        term = lax.dot_general(
            aa[quarters[s]], bb[quarters[s]], NT, preferred_element_type=F32
        )
        if s == 0:
            acc[...] = term
        elif s < 3:
            acc[...] += term
        else:
            corr_v[...] = ((acc[...] + term) * (1.0 / 32.0)).astype(BF16)

    def spread_out(s):
        @pl.when(is_root)
        def _():
            b1_in(s, 0).wait()
            b1_in(s, 1).wait()
            for dy in (1, 3, 2):
                down(s, dy).start()

        @pl.when(jnp.logical_not(is_root))
        def _():
            down(s, 1).wait_recv()

        to_right(s).start()
        to_left(s).start()

    def pass_on(s):
        from_left(s).wait_recv()
        from_right(s).wait_recv()
        forward(s).start()

    def cross(i):
        frm = lax.rem(xy + 16 - i, 16)
        return remote(near_in.at[frm, 1], twin_in.at[frm], fw_s.at[i], fw_r.at[i], twin)

    def cross_step(i, carry):
        plane_in(i).wait_recv()
        cross(i).start()
        return carry

    spread_out(0)
    aa[h, half, :] = activation(1)
    for cp in a_out:
        cp.start()
    relay(0).start()
    spread_out(1)
    pass_on(0)
    own_cross.start()
    lax.fori_loop(1, 16, cross_step, 0)
    spread_out(2)
    for d in (1, 3):
        a_in(d).wait_recv()
        relay(d).start()
    pass_on(1)
    a_in(2).wait_recv()
    relay(2).start()
    spread_out(3)
    pass_on(2)
    for d in range(4):
        relay_in(d).wait_recv()
    from_far(0).wait_recv()
    correlate(0)
    from_far(1).wait_recv()
    correlate(1)
    pass_on(3)
    from_far(2).wait_recv()
    correlate(2)

    own_rows.wait()

    def arrived(i, carry):
        cross(i).wait_recv()
        return carry

    own_cross.wait_recv()
    lax.fori_loop(1, 16, arrived, 0)
    for cp in loads_a:
        cp.wait()
    weight = column[0:UNITS, 1:2]
    outs = []
    for i, out in enumerate((merged_gate, merged_up)):
        got = jnp.dot(
            take_hot[:, : 16 * SLOTS],
            near_in[:, 0, i].reshape(16 * SLOTS, WIDTH),
            preferred_element_type=F32,
        ) + jnp.dot(
            take_hot[:, 16 * SLOTS :],
            twin_in[:, i].reshape(16 * SLOTS, WIDTH),
            preferred_element_type=F32,
        )
        mg_v[i] = ((1.0 - weight) * wa[i].astype(F32) + weight * got).astype(BF16)
        outs.append(pltpu.make_async_copy(mg_v.at[i], out, o_sem.at[i]))
        outs[-1].start()

    from_far(3).wait_recv()
    correlate(3)
    outs.append(pltpu.make_async_copy(corr_v, corr, o_sem.at[2]))
    outs[-1].start()

    for cp in swaps + [to_twin, own_cross] + a_out:
        cp.wait_send()
    for k in range(2):
        for i in range(6):
            ring(k, i).wait_send()

    @pl.when(jnp.logical_not(is_self))
    def _():
        to_root.wait_send()

    for s in range(4):

        @pl.when(is_root)
        def _():
            for dy in (1, 3, 2):
                down(s, dy).wait_send()

        to_right(s).wait_send()
        to_left(s).wait_send()
        forward(s).wait_send()
        relay(s).wait_send()

    def left_all(i, carry):
        plane(i).wait_send()
        cross(i).wait_send()
        return carry

    lax.fori_loop(1, 16, left_all, 0)
    for cp in outs:
        cp.wait()


def body(tokens, gate_a, up_a, gate_b, up_b, matching, mixing):
    any_space = pl.BlockSpec(memory_space=pl.ANY)
    vmem = pl.BlockSpec(memory_space=pltpu.VMEM)
    dma = pltpu.SemaphoreType.DMA
    return pl.pallas_call(
        kernel,
        name="match_merge",
        out_shape=(
            jax.ShapeDtypeStruct((UNITS, 4 * UNITS), BF16),
            jax.ShapeDtypeStruct((UNITS, WIDTH), BF16),
            jax.ShapeDtypeStruct((UNITS, WIDTH), BF16),
        ),
        in_specs=[any_space] * 5 + [vmem] * 2,
        out_specs=(any_space,) * 3,
        scratch_shapes=[
            pltpu.VMEM((2, 1024, WIDTH), BF16),
            pltpu.VMEM((2, 4 * HALF, WIDTH), BF16),
            pltpu.VMEM((2, UNITS, WIDTH), BF16),
            pltpu.VMEM((2, UNITS, WIDTH), BF16),
            pltpu.VMEM((16, 2, 2, SLOTS, WIDTH), BF16),
            pltpu.VMEM((16, 2, 2, SLOTS, WIDTH), BF16),
            pltpu.VMEM((16, 2, SLOTS, WIDTH), BF16),
            pltpu.VMEM((2, 6, HALF, QUARTER), BF16),
            pltpu.VMEM((2, 6, HALF, QUARTER), BF16),
            pltpu.VMEM((2, 4, HALF, QUARTER), F32),
            pltpu.VMEM((HALF, QUARTER), BF16),
            pltpu.VMEM((4, UNITS, QUARTER), BF16),
            pltpu.VMEM((4, 4 * UNITS, QUARTER), BF16),
            pltpu.VMEM((UNITS, 4 * UNITS), F32),
            pltpu.VMEM((UNITS, 4 * UNITS), BF16),
            pltpu.VMEM((2, UNITS, WIDTH), BF16),
            pltpu.VMEM((32 * SLOTS, UNITS), BF16),
            pltpu.VMEM((UNITS, 32 * SLOTS), BF16),
            pltpu.VMEM((8, 512), F32),
            pltpu.VMEM((512, 8), F32),
            pltpu.VMEM((32, UNITS), jnp.int32),
            dma((10,)),
            dma((8,)),
            dma((8,)),
            dma((16,)),
            dma((16,)),
            dma((16,)),
            dma((16,)),
            dma((2, 6)),
            dma((2, 6)),
            dma((2,)),
            dma((8,)),
            dma((4, 3)),
            dma((4,)),
            dma((4, 3)),
            dma((4, 3)),
            dma((4,)),
            dma((4,)),
            dma((4,)),
            dma((4,)),
            dma((3,)),
        ],
        compiler_params=pltpu.CompilerParams(
            collective_id=0, has_side_effects=True, vmem_limit_bytes=56 * 2**20
        ),
        cost_estimate=pl.CostEstimate(
            flops=8_000_000_000, bytes_accessed=20_000_000, transcendentals=500_000
        ),
    )(tokens, gate_a, up_a, gate_b, up_b, matching.reshape(112, 128), mixing.reshape(1, UNITS))


def solution(mesh):
    placed = (
        P(None, "tok"),
        P("fsdp", "tok"),
        P("fsdp", "tok"),
        P("fsdp", "tok"),
        P("fsdp", "tok"),
        P(),
        P("fsdp"),
    )
    return jax.shard_map(
        body,
        mesh=mesh,
        in_specs=placed,
        out_specs=(P("fsdp", "tok"), P("fsdp", "tok"), P("fsdp", "tok")),
        check_vma=False,
    )
```
